32 devices in a mesh: ctx: 8 (over z, y), head: 4 (over x, core).
Axes of the slice: x: 2, y: 2, z: 4, core: 2. Of those that a mesh axis runs over, the one named last changes fastest.
Arguments:
- queries: bfloat16 [16384, 8192], P('ctx', 'head'), may hold values from -9 to 9
- keys: bfloat16 [16384, 1024], P('ctx', 'head'), may hold values from -8 to 8
- values: bfloat16 [16384, 1024], P('ctx', 'head'), may hold values from -6 to 6
- source_block: int32 [128], replicated, may hold values from 0 to 127, as said below
- doc_of_block: int32 [128], replicated, may hold values from 0 to 27, never falling along the last dimension, each value on 1 to 8 neighbouring positions
Outputs:
- attended: bfloat16 [16384, 8192], P(('ctx', 'head'))
The draws below stay inside these ranges and needn't reach their ends.
Inputs may be any that keep to these rules, and one draw needn't show every extreme that they name: `source_block`: each number once. Generation row block b belongs to generation owner b // 16; pack block p lies on context shard p // 16; a context shard receives at most 2 blocks from one generation owner. `doc_of_block`: never falling along the pack; a rollout covers 1 to 8 blocks.
All inputs are finite; a program needn't handle non-finite values.
Results may differ from the reference program's by a relative error of at most 0.008.
Values may be sent and summed in bfloat16 or wider, within the bound.
A program may use at most 64 MiB of HBM per device.

```python
import math
import jax
import jax.numpy as jnp
import numpy as np
from jax import lax

QUERY_HEADS = 64
KEY_VALUE_HEADS = 8
HEAD_SIZE = 128
TOK_DEV = 2048
BLK = 128
DOCMAX = 8
PACK_TOKENS = 16384
NB = 128
DOCS = 28
N_CTX = 8


def newest_values(key, shape):
    return jnp.clip(jax.random.normal(key, shape, jnp.float32), -6.0, 6.0)


def draw_queries(key, part):
    fresh_keys = newest_values(jax.random.fold_in(key, 1), (PACK_TOKENS, QUERY_HEADS * HEAD_SIZE))
    return fresh_keys.astype(jnp.bfloat16)


def draw_keys(key, part):
    fresh_keys = newest_values(jax.random.fold_in(key, 2), (PACK_TOKENS, KEY_VALUE_HEADS * HEAD_SIZE))
    return fresh_keys.astype(jnp.bfloat16)


def draw_source_block(key, part):
    per_shard = TOK_DEV // BLK
    shards = N_CTX
    capacity = max(1, per_shard // shards)
    pair_count = per_shard // capacity
    offset_key, label_key, slot_key, order_key = jax.random.split(key, 4)
    offsets = jax.random.permutation(offset_key, shards)[:pair_count]
    relabel = jax.random.permutation(label_key, shards)
    slot_scores = jax.random.randint(slot_key, (shards, per_shard), 0, 1024) * per_shard + jnp.arange(per_shard)[None, :]
    slot_perm = jnp.argsort(slot_scores, axis=1, stable=True)
    pair_index = slot_perm // capacity
    shard_ids = jnp.arange(shards)[:, None]
    owner_of = jnp.take(relabel, (shard_ids + jnp.take(offsets, pair_index)) % shards).reshape(-1)
    order_keys = jax.random.permutation(order_key, NB)
    same_owner = owner_of[:, None] == owner_of[None, :]
    before = order_keys[None, :] < order_keys[:, None]
    local_of = jnp.sum(same_owner & before, axis=1)
    return (owner_of * per_shard + local_of).astype(jnp.int32)


def steps_of(rng, extent, cuts, least, high):
    factor_of = 1.0
    for dim, blocks in cuts:
        heights = jax.random.uniform(jax.random.fold_in(jax.random.fold_in(rng, 6), dim), (blocks,), jnp.float32, least / len(cuts), high / len(cuts))
        factor_of = factor_of * jnp.repeat(jnp.exp(heights), extent[dim] // blocks).reshape((-1,) + (1,) * (len(extent) - 1 - dim))
    return factor_of


def profile(amount, total, bound, slope):
    loads = [(1 << 20) // math.isqrt(standing ** slope) + 1 for standing in range(2, amount + 1)]
    surplus, counts = total - bound - (amount - 1), [1] * (amount - 1)
    while surplus > 0:
        movable = [i for i in range(amount - 1) if counts[i] < bound]
        mass, left = sum([loads[i] for i in movable]), surplus
        for i in movable:
            extra = min(bound - counts[i], max(1, left * loads[i] // mass), surplus)
            counts[i] = counts[i] + extra
            surplus = surplus - extra
    return np.array([bound] + counts)


def uneven(own_key, number_of, total, limit, lean):
    if number_of == 2:
        one = jax.random.randint(own_key, (), max(1, total - limit), min(limit, total - 1) + 1)
        return jnp.stack([one, total - one])
    lengths = jnp.asarray(profile(number_of, total, limit, lean), jnp.int32)
    pairs = (number_of - 1) // 2
    donor, taker = lengths[1:1 + 2 * pairs:2], lengths[2:2 + 2 * pairs:2]
    room = jnp.minimum(donor - 1, limit - taker)
    shifted = jax.random.randint(jax.random.fold_in(own_key, 1), (pairs,), 0, 1 << 20) % (room + 1)
    lengths = lengths.at[1:1 + 2 * pairs:2].set(donor - shifted).at[2:2 + 2 * pairs:2].set(taker + shifted)
    return lengths[jax.random.permutation(jax.random.fold_in(own_key, 2), number_of)]


def centred(rng, shape, scale, bound, cuts=(), kind=jnp.bfloat16):
    values = scale * jax.random.normal(rng, shape, jnp.float32)
    if cuts:
        values = values * steps_of(rng, shape, cuts, -0.22, 0.18)
    return jnp.clip(values, -bound, bound).astype(kind)


def setup_inputs(seed: int = 0) -> dict:
    key_of = jax.random.split(jax.random.key(seed), 6)
    return {
        "queries": draw_queries(jax.random.fold_in(key_of[5], 71), 0),
        "keys": draw_keys(jax.random.fold_in(key_of[5], 71), 0),
        "values": centred(key_of[2], (PACK_TOKENS, KEY_VALUE_HEADS * HEAD_SIZE), 1.0, 6.0, ((0, 8), (1, 4))),
        "source_block": draw_source_block(jax.random.fold_in(key_of[5], 71), 0),
        "doc_of_block": jnp.searchsorted(jnp.cumsum(uneven(key_of[4], DOCS, NB, DOCMAX, 2)), jnp.arange(NB), side="right").astype(jnp.int32),
    }


def attend(query_block, key_window, value_window, window_docs):
    window = DOCMAX * BLK
    key_pos = jnp.arange(window)
    query_pos = (DOCMAX - 1) * BLK + jnp.arange(BLK)
    causal = key_pos[None, :] <= query_pos[:, None]
    same_doc = window_docs == window_docs[DOCMAX - 1]
    allowed = causal & same_doc[key_pos // BLK][None, :]
    scores = jnp.einsum("qngd,knd->ngqk", query_block.astype(jnp.float32), key_window.astype(jnp.float32)) * (HEAD_SIZE ** -0.5)
    masked = jnp.where(allowed, scores, -1e30)
    row_max = jnp.max(masked, axis=-1, keepdims=True)
    expo_terms = jnp.where(allowed, jnp.exp(masked - row_max), 0.0)
    weights = (expo_terms / jnp.sum(expo_terms, axis=-1, keepdims=True)).astype(jnp.bfloat16)
    mixed_out = jnp.einsum("ngqk,knd->qngd", weights.astype(jnp.float32), value_window.astype(jnp.float32))
    return mixed_out.astype(jnp.bfloat16)


def reference(queries, keys, values, source_block, doc_of_block):
    query_group_size = QUERY_HEADS // KEY_VALUE_HEADS

    def repacked_tokens(array):
        blocks = array.reshape(NB, BLK, array.shape[1])
        return jnp.take(blocks, source_block.astype(jnp.int32), axis=0).reshape(PACK_TOKENS, array.shape[1])

    packed_queries = repacked_tokens(queries).reshape(PACK_TOKENS, KEY_VALUE_HEADS, query_group_size, HEAD_SIZE)
    packed_keys = repacked_tokens(keys).reshape(PACK_TOKENS, KEY_VALUE_HEADS, HEAD_SIZE)
    packed_values = repacked_tokens(values).reshape(PACK_TOKENS, KEY_VALUE_HEADS, HEAD_SIZE)
    reachable_rows = (DOCMAX - 1) * BLK
    key_extended = jnp.concatenate([jnp.zeros((reachable_rows, KEY_VALUE_HEADS, HEAD_SIZE), packed_keys.dtype), packed_keys], axis=0)
    value_extended = jnp.concatenate([jnp.zeros((reachable_rows, KEY_VALUE_HEADS, HEAD_SIZE), packed_values.dtype), packed_values], axis=0)
    doc_ext = jnp.concatenate([jnp.full((DOCMAX - 1,), -1, jnp.int32), doc_of_block.astype(jnp.int32)])

    def one_block(block_index):
        row_start = block_index * BLK
        query_block = lax.dynamic_slice_in_dim(packed_queries, row_start, BLK, 0)
        key_window = lax.dynamic_slice_in_dim(key_extended, row_start, DOCMAX * BLK, 0)
        value_window = lax.dynamic_slice_in_dim(value_extended, row_start, DOCMAX * BLK, 0)
        window_docs = lax.dynamic_slice_in_dim(doc_ext, block_index, DOCMAX, 0)
        return attend(query_block, key_window, value_window, window_docs)

    stacked = lax.map(one_block, jnp.arange(NB, dtype=jnp.int32))
    return stacked.reshape(PACK_TOKENS, QUERY_HEADS * HEAD_SIZE)
```

```python
import functools

import jax
import jax.numpy as jnp
from jax import lax
from jax.experimental import pallas as pl
from jax.experimental.pallas import tpu as pltpu
from jax.sharding import PartitionSpec as P

HEAD_SIZE = 128
BLK = 128
DOCMAX = 8
REACH = DOCMAX - 1
HEADS_PER_CHUNK = 2
LOOKAHEAD = 2
LOG2E = 1.4426950408889634


def kernel(dims, source_ref, doc_ref, queries, keys, values, out, *scratch):
    shards, groups, blocks, cap, kv_heads, chunks, width, kv_width, group_size = dims
    units = 2 + chunks
    scratch = list(scratch)

    def take(count):
        taken = scratch[:count]
        del scratch[:count]
        return taken

    local = take(units)
    outgoing = take(units)
    incoming = take(units)
    (key_ext, value_ext, stage, result, send_table, take_table, reach_table) = take(7)
    (load_sem, own_sem, send_sem, recv_sem, shift_send, shift_recv, out_send, out_recv) = take(8)

    me = lax.axis_index("ctx")
    my_group = lax.axis_index("head")
    quarter = blocks // groups

    def load(unit):
        if unit == 0:
            source = keys
        elif unit == 1:
            source = values
        else:
            source = queries.at[:, :, pl.ds((unit - 2) * width, width)]
        return pltpu.make_async_copy(source, local[unit], load_sem.at[unit])

    for unit in range(units):
        load(unit).start()

    barrier = pltpu.get_barrier_semaphore()

    def greet_shard(step, carry):
        pl.semaphore_signal(barrier, inc=1, device_id={"ctx": lax.rem(me + step, shards)},
                            device_id_type=pl.DeviceIdType.MESH)
        return carry

    def greet_group(step, carry):
        pl.semaphore_signal(barrier, inc=1, device_id={"head": lax.rem(my_group + step, groups)},
                            device_id_type=pl.DeviceIdType.MESH)
        return carry

    lax.fori_loop(1, shards, greet_shard, 0)
    lax.fori_loop(1, groups, greet_group, 0)

    def fill_send(shard, carry):
        picks = [jnp.int32(0)] * cap
        count = jnp.int32(0)
        for i in range(blocks):
            number = source_ref[shard * blocks + i]
            mine = lax.div(number, blocks) == me
            place = lax.rem(number, blocks)
            for r in range(cap):
                picks[r] = jnp.where(mine & (count == r), place, picks[r])
            count = count + jnp.where(mine, 1, 0)
        for r in range(cap):
            send_table[shard * cap + r] = picks[r]
        return carry

    lax.fori_loop(0, shards, fill_send, 0)

    owners = [lax.div(source_ref[me * blocks + i], blocks) for i in range(blocks)]
    for i in range(blocks):
        rank = jnp.int32(0)
        for j in range(i):
            rank = rank + jnp.where(owners[j] == owners[i], 1, 0)
        take_table[i] = owners[i] * cap + rank

    def fill_reach(i, carry):
        block = me * blocks + i
        mine = doc_ref[block]
        count = jnp.int32(0)
        for back in range(1, DOCMAX):
            other = doc_ref[jnp.maximum(block - back, 0)]
            count = count + jnp.where((block - back >= 0) & (other == mine), 1, 0)
        reach_table[i] = (REACH - count) * BLK
        return carry

    lax.fori_loop(0, blocks, fill_reach, 0)

    pl.semaphore_wait(barrier, shards - 1 + groups - 1)

    def send_copy(unit, shard):
        return pltpu.make_async_remote_copy(
            src_ref=outgoing[unit].at[pl.ds(shard * cap, cap)],
            dst_ref=incoming[unit].at[pl.ds(me * cap, cap)],
            send_sem=send_sem.at[unit, shard],
            recv_sem=recv_sem.at[unit, me],
            device_id={"ctx": shard},
            device_id_type=pl.DeviceIdType.MESH,
        )

    def arrival(unit, shard):
        return pltpu.make_async_remote_copy(
            src_ref=outgoing[unit].at[pl.ds(shard * cap, cap)],
            dst_ref=incoming[unit].at[pl.ds(shard * cap, cap)],
            send_sem=send_sem.at[unit, shard],
            recv_sem=recv_sem.at[unit, shard],
            device_id={"ctx": shard},
            device_id_type=pl.DeviceIdType.MESH,
        )

    def own_copy(unit):
        return pltpu.make_async_copy(
            outgoing[unit].at[pl.ds(me * cap, cap)],
            incoming[unit].at[pl.ds(me * cap, cap)],
            own_sem.at[unit],
        )

    def start_unit(unit):
        load(unit).wait()

        def gather(step, carry):
            shard = lax.rem(me + step, shards)
            for r in range(cap):
                slot = shard * cap + r
                outgoing[unit][slot] = local[unit][send_table[slot]]

            @pl.when(step < shards)
            def _():
                send_copy(unit, shard).start()

            return carry

        lax.fori_loop(1, shards + 1, gather, 0)
        own_copy(unit).start()

    def await_unit(unit):
        own_copy(unit).wait()

        def wait(step, carry):
            arrival(unit, lax.rem(me + step, shards)).wait_recv()
            return carry

        lax.fori_loop(1, shards, wait, 0)

    def await_sent(unit):
        def wait(step, carry):
            send_copy(unit, lax.rem(me + step, shards)).wait_send()
            return carry

        lax.fori_loop(1, shards, wait, 0)

    for unit in range(min(2 + LOOKAHEAD, units)):
        start_unit(unit)

    def shift_copy(index, ext, direction):
        return pltpu.make_async_remote_copy(
            src_ref=ext.at[:, pl.ds(blocks, REACH)],
            dst_ref=ext.at[:, pl.ds(0, REACH)],
            send_sem=shift_send.at[index],
            recv_sem=shift_recv.at[index],
            device_id={"ctx": me + direction},
            device_id_type=pl.DeviceIdType.MESH,
        )

    for index, ext in enumerate((key_ext, value_ext)):
        await_unit(index)

        def assemble(i, carry):
            block = incoming[index][take_table[i]]
            for h in range(kv_heads):
                ext[h, REACH + i] = block[:, h * HEAD_SIZE:(h + 1) * HEAD_SIZE]
            return carry

        lax.fori_loop(0, blocks, assemble, 0)

        @pl.when(me < shards - 1)
        def _():
            shift_copy(index, ext, 1).start()

        @pl.when(me == 0)
        def _():
            ext[:, 0:REACH] = jnp.zeros((kv_heads, REACH, BLK, HEAD_SIZE), ext.dtype)

    for index, ext in enumerate((key_ext, value_ext)):
        @pl.when(me > 0)
        def _():
            shift_copy(index, ext, -1).wait_recv()

    def out_copy(chunk, group):
        return pltpu.make_async_remote_copy(
            src_ref=result.at[chunk, group],
            dst_ref=out.at[:, :, pl.ds(my_group * (chunks * width) + chunk * width, width)],
            send_sem=out_send.at[chunk, group],
            recv_sem=out_recv.at[chunk, my_group],
            device_id={"head": group},
            device_id_type=pl.DeviceIdType.MESH,
        )

    def out_arrival(chunk, group):
        return pltpu.make_async_remote_copy(
            src_ref=result.at[chunk, group],
            dst_ref=out.at[:, :, pl.ds(group * (chunks * width) + chunk * width, width)],
            send_sem=out_send.at[chunk, group],
            recv_sem=out_recv.at[chunk, group],
            device_id={"head": group},
            device_id_type=pl.DeviceIdType.MESH,
        )

    def out_own(chunk):
        return pltpu.make_async_copy(
            result.at[chunk, my_group],
            out.at[:, :, pl.ds(my_group * (chunks * width) + chunk * width, width)],
            out_send.at[chunk, my_group],
        )

    heads = width // HEAD_SIZE
    rows = heads * BLK
    window = DOCMAX * BLK
    factor = HEAD_SIZE ** -0.5 * LOG2E

    def group_at(step):
        chips = groups // 2
        chip, core = my_group // 2, lax.rem(my_group, 2)
        return (lax.rem(chip + chips - 1 - step // 2 + chips, chips) * 2
                + lax.rem(core + 1 + step, 2))

    def one_chunk(chunk, carry):
        for k in range(chunks):
            @pl.when(chunk == k)
            def _():
                await_unit(2 + k)
                if 2 + k + LOOKAHEAD < units:
                    start_unit(2 + k + LOOKAHEAD)

                def move(i, inner):
                    stage[i] = incoming[2 + k][take_table[i]]
                    return inner

                lax.fori_loop(0, blocks, move, 0)

        kv = (chunk * heads) // group_size

        def one_group(step, inner):
            group = group_at(step)

            def one_block(j, deep):
                block = group * quarter + j
                query = stage[block]
                query = jnp.concatenate(
                    [query[:, h * HEAD_SIZE:(h + 1) * HEAD_SIZE] for h in range(heads)], axis=0)
                key = key_ext[kv, pl.ds(block, DOCMAX)].reshape(window, HEAD_SIZE)
                value = value_ext[kv, pl.ds(block, DOCMAX)].reshape(window, HEAD_SIZE)
                scores = lax.dot_general(query, key, (((1,), (1,)), ((), ())),
                                         preferred_element_type=jnp.float32)
                column = lax.broadcasted_iota(jnp.int32, (rows, window), 1)
                row = lax.rem(lax.broadcasted_iota(jnp.int32, (rows, window), 0), BLK)
                allowed = (column >= reach_table[block]) & (column <= row + REACH * BLK)
                scores = jnp.where(allowed, scores, -1e30)
                top = jnp.max(scores, axis=1, keepdims=True)
                terms = jnp.exp2((scores - top) * factor)
                total = jnp.sum(terms, axis=1, keepdims=True)
                mixed = jnp.dot(terms.astype(jnp.bfloat16), value,
                                preferred_element_type=jnp.float32)
                mixed = (mixed / total).astype(jnp.bfloat16)
                for h in range(heads):
                    result[chunk, group, j, :, h * HEAD_SIZE:(h + 1) * HEAD_SIZE] = (
                        mixed[h * BLK:(h + 1) * BLK])
                return deep

            lax.fori_loop(0, quarter, one_block, 0)

            @pl.when(step < groups - 1)
            def _():
                out_copy(chunk, group).start()

            @pl.when(step == groups - 1)
            def _():
                out_own(chunk).start()

            return inner

        lax.fori_loop(0, groups, one_group, 0)
        return carry

    lax.fori_loop(0, chunks, one_chunk, 0)

    for unit in range(units):
        await_sent(unit)

    for index, ext in enumerate((key_ext, value_ext)):
        @pl.when(me < shards - 1)
        def _():
            shift_copy(index, ext, 1).wait_send()

    def finish(chunk, carry):
        out_own(chunk).wait()

        def wait(step, inner):
            group = lax.rem(my_group + step, groups)
            out_copy(chunk, group).wait_send()
            out_arrival(chunk, group).wait_recv()
            return inner

        lax.fori_loop(1, groups, wait, 0)
        return carry

    lax.fori_loop(0, chunks, finish, 0)


def local(queries, keys, values, source_block, doc_of_block):
    shards = lax.axis_size("ctx")
    groups = lax.axis_size("head")
    row_count, query_width = queries.shape
    kv_width = keys.shape[1]
    blocks = row_count // BLK
    cap = max(1, blocks // shards)
    kv_heads = kv_width // HEAD_SIZE
    group_size = query_width // kv_width
    width = HEADS_PER_CHUNK * HEAD_SIZE
    chunks = query_width // width
    units = 2 + chunks
    quarter = blocks // groups
    dims = (shards, groups, blocks, cap, kv_heads, chunks, width, kv_width, group_size)
    kind = queries.dtype
    widths = [kv_width, kv_width] + [width] * chunks
    anywhere = pl.BlockSpec(memory_space=pl.ANY)
    scalars = pl.BlockSpec(memory_space=pltpu.SMEM)
    dma = pltpu.SemaphoreType.DMA
    out = pl.pallas_call(
        functools.partial(kernel, dims),
        out_shape=jax.ShapeDtypeStruct((quarter, BLK, groups * query_width), kind),
        in_specs=[scalars, scalars, anywhere, anywhere, anywhere],
        out_specs=anywhere,
        scratch_shapes=(
            [pltpu.VMEM((blocks, BLK, w), kind) for w in widths]
            + [pltpu.VMEM((shards * cap, BLK, w), kind) for w in widths]
            + [pltpu.VMEM((shards * cap, BLK, w), kind) for w in widths]
            + [pltpu.VMEM((kv_heads, REACH + blocks, BLK, HEAD_SIZE), kind)] * 2
            + [
                pltpu.VMEM((blocks, BLK, width), kind),
                pltpu.VMEM((chunks, groups, quarter, BLK, width), kind),
                pltpu.SMEM((shards * cap,), jnp.int32),
                pltpu.SMEM((blocks,), jnp.int32),
                pltpu.SMEM((blocks,), jnp.int32),
                dma((units,)),
                dma((units,)),
                dma((units, shards)),
                dma((units, shards)),
                dma((2,)),
                dma((2,)),
                dma((chunks, groups)),
                dma((chunks, groups)),
            ]
        ),
        compiler_params=pltpu.CompilerParams(
            collective_id=0, has_side_effects=True, vmem_limit_bytes=58 * 1024 * 1024
        ),
    )(
        source_block,
        doc_of_block,
        queries.reshape(blocks, BLK, query_width),
        keys.reshape(blocks, BLK, kv_width),
        values.reshape(blocks, BLK, kv_width),
    )
    return out.reshape(row_count // groups, groups * query_width)


def solution(mesh):
    in_specs = (P("ctx", "head"), P("ctx", "head"), P("ctx", "head"), P(), P())
    out_specs = P(("ctx", "head"), None)
    return jax.shard_map(local, mesh=mesh, in_specs=in_specs, out_specs=out_specs, check_vma=False)
```

```python
import functools

import jax
import jax.numpy as jnp
from jax import lax
from jax.experimental import pallas as pl
from jax.experimental.pallas import tpu as pltpu
from jax.sharding import PartitionSpec as P

HEAD_SIZE = 128
BLK = 128
DOCMAX = 8
REACH = DOCMAX - 1
HEADS_PER_CHUNK = 2
LOOKAHEAD = 2
LOG2E = 1.4426950408889634


def kernel(dims, source_ref, doc_ref, queries, keys, values, out, *scratch):
    shards, groups, blocks, cap, kv_heads, chunks, width, kv_width, group_size = dims
    units = 2 + chunks
    scratch = list(scratch)

    def take(count):
        taken = scratch[:count]
        del scratch[:count]
        return taken

    local = take(units)
    outgoing = take(units)
    incoming = take(units)
    (key_ext, value_ext, relay, stage, result, send_table, take_table, reach_table) = take(8)
    (load_sem, own_sem, send_sem, recv_sem, shift_send, shift_recv, relay_sem,
     out_send, out_recv) = take(9)

    me = lax.axis_index("ctx")
    my_group = lax.axis_index("head")
    quarter = blocks // groups

    def load(unit):
        if unit == 0:
            source = keys
        elif unit == 1:
            source = values
        else:
            source = queries.at[:, :, pl.ds((unit - 2) * width, width)]
        return pltpu.make_async_copy(source, local[unit], load_sem.at[unit])

    for unit in range(units):
        load(unit).start()

    barrier = pltpu.get_barrier_semaphore()

    def greet_shard(step, carry):
        pl.semaphore_signal(barrier, inc=1, device_id={"ctx": lax.rem(me + step, shards)},
                            device_id_type=pl.DeviceIdType.MESH)
        return carry

    def greet_group(step, carry):
        pl.semaphore_signal(barrier, inc=1, device_id={"head": lax.rem(my_group + step, groups)},
                            device_id_type=pl.DeviceIdType.MESH)
        return carry

    lax.fori_loop(1, shards, greet_shard, 0)
    lax.fori_loop(1, groups, greet_group, 0)

    def fill_send(shard, carry):
        picks = [jnp.int32(0)] * cap
        count = jnp.int32(0)
        for i in range(blocks):
            number = source_ref[shard * blocks + i]
            mine = lax.div(number, blocks) == me
            place = lax.rem(number, blocks)
            for r in range(cap):
                picks[r] = jnp.where(mine & (count == r), place, picks[r])
            count = count + jnp.where(mine, 1, 0)
        for r in range(cap):
            send_table[shard * cap + r] = picks[r]
        return carry

    lax.fori_loop(0, shards, fill_send, 0)

    pl.semaphore_wait(barrier, shards - 1 + groups - 1)

    def send_copy(unit, shard):
        return pltpu.make_async_remote_copy(
            src_ref=outgoing[unit].at[pl.ds(shard * cap, cap)],
            dst_ref=incoming[unit].at[pl.ds(me * cap, cap)],
            send_sem=send_sem.at[unit, shard],
            recv_sem=recv_sem.at[unit, me],
            device_id={"ctx": shard},
            device_id_type=pl.DeviceIdType.MESH,
        )

    def arrival(unit, shard):
        return pltpu.make_async_remote_copy(
            src_ref=outgoing[unit].at[pl.ds(shard * cap, cap)],
            dst_ref=incoming[unit].at[pl.ds(shard * cap, cap)],
            send_sem=send_sem.at[unit, shard],
            recv_sem=recv_sem.at[unit, shard],
            device_id={"ctx": shard},
            device_id_type=pl.DeviceIdType.MESH,
        )

    def own_copy(unit):
        return pltpu.make_async_copy(
            outgoing[unit].at[pl.ds(me * cap, cap)],
            incoming[unit].at[pl.ds(me * cap, cap)],
            own_sem.at[unit],
        )

    def start_unit(unit):
        load(unit).wait()

        def gather(step, carry):
            shard = lax.rem(me + step, shards)
            for r in range(cap):
                slot = shard * cap + r
                outgoing[unit][slot] = local[unit][send_table[slot]]

            @pl.when(step < shards)
            def _():
                send_copy(unit, shard).start()

            return carry

        lax.fori_loop(1, shards + 1, gather, 0)
        own_copy(unit).start()

    def await_unit(unit):
        own_copy(unit).wait()

        def wait(step, carry):
            arrival(unit, lax.rem(me + step, shards)).wait_recv()
            return carry

        lax.fori_loop(1, shards, wait, 0)

    def await_sent(unit):
        def wait(step, carry):
            send_copy(unit, lax.rem(me + step, shards)).wait_send()
            return carry

        lax.fori_loop(1, shards, wait, 0)

    for unit in range(min(2 + LOOKAHEAD, units)):
        start_unit(unit)

    owners = [lax.div(source_ref[me * blocks + i], blocks) for i in range(blocks)]
    for i in range(blocks):
        rank = jnp.int32(0)
        for j in range(i):
            rank = rank + jnp.where(owners[j] == owners[i], 1, 0)
        take_table[i] = owners[i] * cap + rank

    def fill_reach(i, carry):
        block = me * blocks + i
        mine = doc_ref[block]
        count = jnp.int32(0)
        for back in range(1, DOCMAX):
            other = doc_ref[jnp.maximum(block - back, 0)]
            count = count + jnp.where((block - back >= 0) & (other == mine), 1, 0)
        reach_table[i] = (REACH - count) * BLK
        return carry

    lax.fori_loop(0, blocks, fill_reach, 0)

    def shift_copy(index, ext, direction):
        return pltpu.make_async_remote_copy(
            src_ref=ext.at[:, pl.ds(blocks, REACH)],
            dst_ref=ext.at[:, pl.ds(0, REACH)],
            send_sem=shift_send.at[index],
            recv_sem=shift_recv.at[index],
            device_id={"ctx": me + direction},
            device_id_type=pl.DeviceIdType.MESH,
        )

    first_hop, second_hop = -1, 2
    relays = (me % 2 == 1) & (me < shards - 1)
    forwards = ((me - first_hop) % 2 == 1) & (me - first_hop > 0) & (me - first_hop < shards - 1)

    def relay_copy():
        return pltpu.make_async_remote_copy(
            src_ref=value_ext.at[:, pl.ds(blocks, REACH)],
            dst_ref=relay,
            send_sem=relay_sem.at[0],
            recv_sem=relay_sem.at[1],
            device_id={"ctx": me + first_hop},
            device_id_type=pl.DeviceIdType.MESH,
        )

    def forward_copy():
        return pltpu.make_async_remote_copy(
            src_ref=relay,
            dst_ref=value_ext.at[:, pl.ds(0, REACH)],
            send_sem=relay_sem.at[2],
            recv_sem=shift_recv.at[1],
            device_id={"ctx": me + second_hop},
            device_id_type=pl.DeviceIdType.MESH,
        )

    for index, ext in enumerate((key_ext, value_ext)):
        await_unit(index)

        def assemble(i, carry):
            block = incoming[index][take_table[i]]
            for h in range(kv_heads):
                ext[h, REACH + i] = block[:, h * HEAD_SIZE:(h + 1) * HEAD_SIZE]
            return carry

        lax.fori_loop(0, blocks, assemble, 0)

        straight = (me < shards - 1) if index == 0 else (me < shards - 1) & (me % 2 == 0)

        @pl.when(straight)
        def _():
            shift_copy(index, ext, 1).start()

        @pl.when(me == 0)
        def _():
            ext[:, 0:REACH] = jnp.zeros((kv_heads, REACH, BLK, HEAD_SIZE), ext.dtype)

    @pl.when(relays)
    def _():
        relay_copy().start()

    @pl.when(forwards)
    def _():
        relay_copy().wait_recv()
        forward_copy().start()

    for index, ext in enumerate((key_ext, value_ext)):
        @pl.when(me > 0)
        def _():
            shift_copy(index, ext, -1).wait_recv()

    def out_copy(chunk, group):
        return pltpu.make_async_remote_copy(
            src_ref=result.at[chunk, group],
            dst_ref=out.at[:, :, pl.ds(my_group * (chunks * width) + chunk * width, width)],
            send_sem=out_send.at[chunk, group],
            recv_sem=out_recv.at[chunk, my_group],
            device_id={"head": group},
            device_id_type=pl.DeviceIdType.MESH,
        )

    def out_arrival(chunk, group):
        return pltpu.make_async_remote_copy(
            src_ref=result.at[chunk, group],
            dst_ref=out.at[:, :, pl.ds(group * (chunks * width) + chunk * width, width)],
            send_sem=out_send.at[chunk, group],
            recv_sem=out_recv.at[chunk, group],
            device_id={"head": group},
            device_id_type=pl.DeviceIdType.MESH,
        )

    def out_own(chunk):
        return pltpu.make_async_copy(
            result.at[chunk, my_group],
            out.at[:, :, pl.ds(my_group * (chunks * width) + chunk * width, width)],
            out_send.at[chunk, my_group],
        )

    heads = width // HEAD_SIZE
    rows = heads * BLK
    window = DOCMAX * BLK
    factor = HEAD_SIZE ** -0.5 * LOG2E

    def group_at(step):
        chips = groups // 2
        chip, core = my_group // 2, lax.rem(my_group, 2)
        return (lax.rem(chip + chips - 1 - step // 2 + chips, chips) * 2
                + lax.rem(core + 1 + step, 2))

    def one_chunk(chunk, carry):
        for k in range(chunks):
            @pl.when(chunk == k)
            def _():
                await_unit(2 + k)
                if 2 + k + LOOKAHEAD < units:
                    start_unit(2 + k + LOOKAHEAD)

                def move(i, inner):
                    stage[i] = incoming[2 + k][take_table[i]]
                    return inner

                lax.fori_loop(0, blocks, move, 0)

        kv = (chunk * heads) // group_size

        def one_group(step, inner):
            group = group_at(step)

            def one_block(j, deep):
                block = group * quarter + j
                query = stage[block]
                query = jnp.concatenate(
                    [query[:, h * HEAD_SIZE:(h + 1) * HEAD_SIZE] for h in range(heads)], axis=0)
                key = key_ext[kv, pl.ds(block, DOCMAX)].reshape(window, HEAD_SIZE)
                value = value_ext[kv, pl.ds(block, DOCMAX)].reshape(window, HEAD_SIZE)
                scores = lax.dot_general(query, key, (((1,), (1,)), ((), ())),
                                         preferred_element_type=jnp.float32)
                column = lax.broadcasted_iota(jnp.int32, (rows, window), 1)
                row = lax.rem(lax.broadcasted_iota(jnp.int32, (rows, window), 0), BLK)
                allowed = (column >= reach_table[block]) & (column <= row + REACH * BLK)
                scores = jnp.where(allowed, scores, -1e30)
                top = jnp.max(scores, axis=1, keepdims=True)
                terms = jnp.exp2((scores - top) * factor)
                total = jnp.sum(terms, axis=1, keepdims=True)
                mixed = jnp.dot(terms.astype(jnp.bfloat16), value,
                                preferred_element_type=jnp.float32)
                mixed = (mixed / total).astype(jnp.bfloat16)
                for h in range(heads):
                    result[chunk, group, j, :, h * HEAD_SIZE:(h + 1) * HEAD_SIZE] = (
                        mixed[h * BLK:(h + 1) * BLK])
                return deep

            lax.fori_loop(0, quarter, one_block, 0)

            @pl.when(step < groups - 1)
            def _():
                out_copy(chunk, group).start()

            @pl.when(step == groups - 1)
            def _():
                out_own(chunk).start()

            return inner

        lax.fori_loop(0, groups, one_group, 0)
        return carry

    lax.fori_loop(0, chunks, one_chunk, 0)

    for unit in range(units):
        await_sent(unit)

    for index, ext in enumerate((key_ext, value_ext)):
        straight = (me < shards - 1) if index == 0 else (me < shards - 1) & (me % 2 == 0)

        @pl.when(straight)
        def _():
            shift_copy(index, ext, 1).wait_send()

    @pl.when(relays)
    def _():
        relay_copy().wait_send()

    @pl.when(forwards)
    def _():
        forward_copy().wait_send()

    def finish(chunk, carry):
        out_own(chunk).wait()

        def wait(step, inner):
            group = lax.rem(my_group + step, groups)
            out_copy(chunk, group).wait_send()
            out_arrival(chunk, group).wait_recv()
            return inner

        lax.fori_loop(1, groups, wait, 0)
        return carry

    lax.fori_loop(0, chunks, finish, 0)


def local(queries, keys, values, source_block, doc_of_block):
    shards = lax.axis_size("ctx")
    groups = lax.axis_size("head")
    row_count, query_width = queries.shape
    kv_width = keys.shape[1]
    blocks = row_count // BLK
    cap = max(1, blocks // shards)
    kv_heads = kv_width // HEAD_SIZE
    group_size = query_width // kv_width
    width = HEADS_PER_CHUNK * HEAD_SIZE
    chunks = query_width // width
    units = 2 + chunks
    quarter = blocks // groups
    dims = (shards, groups, blocks, cap, kv_heads, chunks, width, kv_width, group_size)
    kind = queries.dtype
    widths = [kv_width, kv_width] + [width] * chunks
    anywhere = pl.BlockSpec(memory_space=pl.ANY)
    scalars = pl.BlockSpec(memory_space=pltpu.SMEM)
    dma = pltpu.SemaphoreType.DMA
    out = pl.pallas_call(
        functools.partial(kernel, dims),
        out_shape=jax.ShapeDtypeStruct((quarter, BLK, groups * query_width), kind),
        in_specs=[scalars, scalars, anywhere, anywhere, anywhere],
        out_specs=anywhere,
        scratch_shapes=(
            [pltpu.VMEM((blocks, BLK, w), kind) for w in widths]
            + [pltpu.VMEM((shards * cap, BLK, w), kind) for w in widths]
            + [pltpu.VMEM((shards * cap, BLK, w), kind) for w in widths]
            + [pltpu.VMEM((kv_heads, REACH + blocks, BLK, HEAD_SIZE), kind)] * 2
            + [
                pltpu.VMEM((kv_heads, REACH, BLK, HEAD_SIZE), kind),
                pltpu.VMEM((blocks, BLK, width), kind),
                pltpu.VMEM((chunks, groups, quarter, BLK, width), kind),
                pltpu.SMEM((shards * cap,), jnp.int32),
                pltpu.SMEM((blocks,), jnp.int32),
                pltpu.SMEM((blocks,), jnp.int32),
                dma((units,)),
                dma((units,)),
                dma((units, shards)),
                dma((units, shards)),
                dma((2,)),
                dma((2,)),
                dma((3,)),
                dma((chunks, groups)),
                dma((chunks, groups)),
            ]
        ),
        compiler_params=pltpu.CompilerParams(
            collective_id=0, has_side_effects=True, vmem_limit_bytes=58 * 1024 * 1024
        ),
    )(
        source_block,
        doc_of_block,
        queries.reshape(blocks, BLK, query_width),
        keys.reshape(blocks, BLK, kv_width),
        values.reshape(blocks, BLK, kv_width),
    )
    return out.reshape(row_count // groups, groups * query_width)


def solution(mesh):
    in_specs = (P("ctx", "head"), P("ctx", "head"), P("ctx", "head"), P(), P())
    out_specs = P(("ctx", "head"), None)
    return jax.shard_map(local, mesh=mesh, in_specs=in_specs, out_specs=out_specs, check_vma=False)
```
